1024 devices in a mesh: outer: 32 (over y, z_hi), inner: 32 (over z_lo, x, core).
Axes of the slice: x: 4, y: 8, z: 16 (z_hi: 4, z_lo: 4; z = z_hi * 4 + z_lo), core: 2. Of those that a mesh axis runs over, the one named last changes fastest.
Arguments:
- image_embeds: bfloat16 [524288, 512], P(('outer', 'inner')), may hold values from -0.17766058 to 0.17766058
- text_embeds: bfloat16 [524288, 512], P(('outer', 'inner')), may hold values from -0.17766058 to 0.17766058
- image_lse: float32 [524288], P(('outer', 'inner')), as said below
- text_lse: float32 [524288], P(('outer', 'inner')), as said below
- logit_scale: float32 [], replicated, may hold values from 90 to 100, as said below
Outputs:
- image_grad: float32 [524288, 512], P(('outer', 'inner'))
- text_grad: float32 [524288, 512], P(('outer', 'inner'))
The draws below stay inside these ranges and needn't reach their ends.
Inputs may be any that keep to these rules, and one draw needn't show every extreme that they name: logit_scale is one positive number. `image_lse`: saved by the forward pass: for image row i, the log of the sum of exp(score_ij) over the text rows j that the window pairs with it. `text_lse`: saved by the forward pass: for text row j, the log of the sum of exp(score_ij) over the image rows i that the window pairs with it.
All inputs are finite; a program needn't handle non-finite values.
Results may differ from the reference program's by a relative error of at most 0.0013.
Values may be sent and summed in bfloat16 or wider, within the bound.
No kernel may reach another device: no remote copies, remote signals or barrier semaphores. Data moves between devices by JAX's collectives and lax.ppermute only.
A program may use at most 32 MiB of HBM per device.

```python
import math
import jax
import jax.numpy as jnp
from jax import lax

E = 512
ROWS = 512
PAIRS = 524288
N_OUTER = 32
N_INNER = 32


def shared_scale(key):
    return 90.0 + 10.0 * jax.random.uniform(jax.random.fold_in(key, 97), (), jnp.float32)


def modality(key, label_id, exponent):
    key = jax.random.fold_in(key, label_id)
    normal_draw = jax.random.normal(key, (PAIRS, E), jnp.float32)
    shaped = jnp.sign(normal_draw) * jnp.abs(normal_draw) ** exponent
    blended = shaped
    return (jnp.clip(blended, -4.0, 4.0) * (1.0 / math.sqrt(E))).astype(jnp.bfloat16)


def window_lse(key, exponent):
    factor = shared_scale(key)
    images = lax.optimization_barrier(modality(key, 101, exponent)).astype(jnp.float32)
    text_rows = lax.optimization_barrier(modality(key, 202, exponent)).astype(jnp.float32)
    images = images.reshape(N_OUTER, N_INNER, ROWS, E)
    text_rows = text_rows.reshape(N_OUTER, N_INNER, ROWS, E)
    left_text = jnp.roll(text_rows, 1, axis=1)
    upper_text = jnp.roll(text_rows, 1, axis=0)
    corner_text = jnp.roll(upper_text, 1, axis=1)

    def one_group(inputs):
        image_block = inputs[0]
        score_tiles = jnp.stack([factor * jnp.einsum('nre,nse->nrs', image_block, text_block, precision=lax.Precision.HIGHEST) for text_block in inputs[1:]], axis=1)
        return (jax.nn.logsumexp(score_tiles, axis=(1, 3)), jax.nn.logsumexp(score_tiles, axis=2))
    row_lse, column_lse = lax.map(one_group, (images, text_rows, left_text, upper_text, corner_text))
    column_parts = jnp.stack([column_lse[:, :, 0], jnp.roll(column_lse[:, :, 1], -1, axis=1), jnp.roll(column_lse[:, :, 2], -1, axis=0), jnp.roll(jnp.roll(column_lse[:, :, 3], -1, axis=0), -1, axis=1)], axis=0)
    text_stat = jax.nn.logsumexp(column_parts, axis=0)
    return (row_lse.reshape(PAIRS), text_stat.reshape(PAIRS))


def draw_logit_scale(key, part):
    return shared_scale(key).astype(jnp.float32)


def draw_image_embeds(key, part):
    return modality(key, 101, 1.0)


def draw_text_embeds(key, part):
    return modality(key, 202, 1.0)


def draw_image_lse(key, part):
    row_lse, text_stat = window_lse(key, 1.0)
    return row_lse.astype(jnp.float32)


def draw_text_lse(key, part):
    row_lse, text_stat = window_lse(key, 1.0)
    return text_stat.astype(jnp.float32)


def setup_inputs(seed: int = 0) -> dict:
    arg_keys = jax.random.split(jax.random.key(seed), 6)
    image_embeds = draw_image_embeds(jax.random.fold_in(arg_keys[5], 71), 0)
    text_embeds = draw_text_embeds(jax.random.fold_in(arg_keys[5], 71), 0)
    image_lse = draw_image_lse(jax.random.fold_in(arg_keys[5], 71), 0)
    text_lse = draw_text_lse(jax.random.fold_in(arg_keys[5], 71), 0)
    logit_scale = draw_logit_scale(jax.random.fold_in(arg_keys[5], 71), 0)
    return dict(image_embeds=image_embeds, text_embeds=text_embeds, image_lse=image_lse, text_lse=text_lse, logit_scale=logit_scale)


def tile_terms(images, image_stat, text_rows, text_stat, factor):
    scores = factor * jnp.einsum("nre,nse->nrs", images.astype(jnp.float32), text_rows.astype(jnp.float32))
    weights = (jnp.exp(scores - image_stat[:, :, None]) + jnp.exp(scores - text_stat[:, None, :])).astype(jnp.bfloat16)
    widened = lax.optimization_barrier(weights).astype(jnp.float32)
    image_term = jnp.einsum("nrs,nse->nre", widened, text_rows.astype(jnp.float32))
    text_term = jnp.einsum("nrs,nre->nse", widened, images.astype(jnp.float32))
    return image_term, text_term


def reference(image_embeds, text_embeds, image_lse, text_lse, logit_scale):
    factor = logit_scale.astype(jnp.float32)
    images = image_embeds.reshape(N_OUTER, N_INNER, ROWS, E)
    text_rows = text_embeds.reshape(N_OUTER, N_INNER, ROWS, E)
    image_stat = image_lse.astype(jnp.float32).reshape(N_OUTER, N_INNER, ROWS)
    text_stat = text_lse.astype(jnp.float32).reshape(N_OUTER, N_INNER, ROWS)
    left_text = jnp.roll(text_rows, 1, axis=1)
    upper_text = jnp.roll(text_rows, 1, axis=0)
    corner_text = jnp.roll(upper_text, 1, axis=1)
    left_stat = jnp.roll(text_stat, 1, axis=1)
    upper_stat = jnp.roll(text_stat, 1, axis=0)
    corner_stat = jnp.roll(upper_stat, 1, axis=1)

    def one_group(inputs):
        image_block, image_here, own_text, own_stat, left_block, left_here, upper_block, upper_here, corner_block, corner_here = inputs
        own_image, own_part = tile_terms(image_block, image_here, own_text, own_stat, factor)
        left_image, left_part = tile_terms(image_block, image_here, left_block, left_here, factor)
        upper_image, upper_part = tile_terms(image_block, image_here, upper_block, upper_here, factor)
        corner_image, corner_part = tile_terms(image_block, image_here, corner_block, corner_here, factor)
        image_total = own_image + left_image + upper_image + corner_image
        same_group = own_part + jnp.roll(left_part, -1, axis=0)
        prior_group = upper_part + jnp.roll(corner_part, -1, axis=0)
        return image_total, same_group, prior_group

    image_total, same_group, prior_group = lax.map(one_group, (images, image_stat, text_rows, text_stat, left_text, left_stat, upper_text, upper_stat, corner_text, corner_stat))
    text_total = same_group + jnp.roll(prior_group, -1, axis=0)
    image_grad = factor * (image_total - 2.0 * text_rows.astype(jnp.float32))
    text_grad = factor * (text_total - 2.0 * images.astype(jnp.float32))
    return image_grad.reshape(PAIRS, E), text_grad.reshape(PAIRS, E)
```

```python
import jax
import jax.numpy as jnp
from jax import lax
from jax.sharding import PartitionSpec as P

PARTS = 1


def shifted(value, axis, steps):
    count = lax.axis_size(axis)
    pairs = [(source, (source + steps) % count) for source in range(count)]
    return lax.ppermute(value, axis, pairs)


def tile_weights(images, image_stat, text_rows, text_stat, factor):
    scores = factor * lax.dot_general(
        images, text_rows, (((1,), (1,)), ((), ())), preferred_element_type=jnp.float32
    )
    return (jnp.exp(scores - image_stat[:, None]) + jnp.exp(scores - text_stat[None, :])).astype(
        jnp.bfloat16
    )


def image_side(weights, text_rows):
    return jnp.dot(weights, text_rows, preferred_element_type=jnp.float32)


def text_side(weights, images):
    return lax.dot_general(
        weights, images, (((0,), (0,)), ((), ())), preferred_element_type=jnp.float32
    )


def local(image_embeds, text_embeds, image_lse, text_lse, logit_scale):
    rows = image_embeds.shape[0]
    size = rows // PARTS
    cuts = [slice(k * size, (k + 1) * size) for k in range(PARTS)]
    far_texts = [shifted(text_embeds[cut], "outer", 1) for cut in cuts]
    far_images = [shifted(image_embeds[cut], "outer", -1) for cut in cuts]
    near_text = shifted(text_embeds, "inner", 1)
    near_image = shifted(image_embeds, "inner", -1)
    far_text_lse = shifted(text_lse, "outer", 1)
    far_image_lse = shifted(image_lse, "outer", -1)
    near_text_lse, both_text_lse = shifted(jnp.stack([text_lse, far_text_lse]), "inner", 1)
    near_image_lse, both_image_lse = shifted(jnp.stack([image_lse, far_image_lse]), "inner", -1)
    both_texts = [shifted(far, "inner", 1) for far in far_texts]
    both_images = [shifted(far, "inner", -1) for far in far_images]

    own = tile_weights(image_embeds, image_lse, text_embeds, text_lse, logit_scale)
    image_total = image_side(own, text_embeds)
    text_total = text_side(own, image_embeds)

    def add_texts(total, texts, stat):
        weights = tile_weights(image_embeds, image_lse, texts, stat, logit_scale)
        return total + image_side(weights, texts)

    def add_images(total, images, stat):
        weights = tile_weights(images, stat, text_embeds, text_lse, logit_scale)
        return total + text_side(weights, images)

    image_total = add_texts(image_total, near_text, near_text_lse)
    text_total = add_images(text_total, near_image, near_image_lse)
    for k, cut in enumerate(cuts):
        image_total = add_texts(image_total, far_texts[k], far_text_lse[cut])
        text_total = add_images(text_total, far_images[k], far_image_lse[cut])
    for k, cut in enumerate(cuts):
        image_total = add_texts(image_total, both_texts[k], both_text_lse[cut])
        text_total = add_images(text_total, both_images[k], both_image_lse[cut])
    image_grad = logit_scale * (image_total - 2.0 * text_embeds.astype(jnp.float32))
    text_grad = logit_scale * (text_total - 2.0 * image_embeds.astype(jnp.float32))
    return (image_grad, text_grad)


def solution(mesh):
    return jax.shard_map(
        local,
        mesh=mesh,
        in_specs=(
            P(("outer", "inner"), None),
            P(("outer", "inner"), None),
            P(("outer", "inner")),
            P(("outer", "inner")),
            P(),
        ),
        out_specs=(P(("outer", "inner"), None), P(("outer", "inner"), None)),
        check_vma=False,
    )
```

```python
import jax
import jax.numpy as jnp
from jax import lax
from jax.experimental import pallas as pl
from jax.experimental.pallas import tpu as pltpu
from jax.sharding import PartitionSpec as P

STAT_ROWS = 16
BLOCKS = 2
VMEM_BYTES = 16 * 1024 * 1024
PACK_VMEM_BYTES = 60 * 1024 * 1024
ON_IMAGES = (2**29, 2**30, 2**29)
ON_TEXTS = (2**29, 2**30, 2**29)


def shifted(value, axis, steps):
    count = lax.axis_size(axis)
    pairs = [(source, (source + steps) % count) for source in range(count)]
    return lax.ppermute(value, axis, pairs)


def pack_kernel(text_ref, text_stat_ref, image_ref, image_stat_ref, text_out, image_out, sems):
    rows = text_ref.shape[0]
    sides = ((text_ref, text_stat_ref, text_out), (image_ref, image_stat_ref, image_out))
    moves = [
        pltpu.make_async_copy(rows_ref, out.at[pl.ds(0, rows), :], sems.at[k])
        for k, (rows_ref, _, out) in enumerate(sides)
    ]
    for copy in moves:
        copy.start()
    for _, stat_ref, out in sides:
        stat = stat_ref[...]
        upper = stat.astype(jnp.bfloat16).astype(jnp.float32)
        rest = stat - upper
        middle = rest.astype(jnp.bfloat16).astype(jnp.float32)
        lower = rest - middle
        zeros = jnp.zeros((STAT_ROWS - 3, stat.shape[1]), jnp.float32)
        out[pl.ds(rows, STAT_ROWS), :] = jnp.concatenate(
            [upper, middle, lower, zeros], axis=0
        ).astype(jnp.bfloat16)
    for copy in moves:
        copy.wait()


def pack(text, text_stat, image, image_stat):
    rows, width = text.shape
    packed = jax.ShapeDtypeStruct((rows + STAT_ROWS, width), jnp.bfloat16)
    hbm = pl.BlockSpec(memory_space=pltpu.HBM)
    vmem = pl.BlockSpec(memory_space=pltpu.VMEM)
    return pl.pallas_call(
        pack_kernel,
        in_specs=[hbm, vmem, hbm, vmem],
        out_specs=(vmem, vmem),
        out_shape=(packed, packed),
        scratch_shapes=[pltpu.SemaphoreType.DMA((2,))],
        compiler_params=pltpu.CompilerParams(vmem_limit_bytes=PACK_VMEM_BYTES),
    )(text, text_stat.reshape(1, rows), image, image_stat.reshape(1, rows))


def tile_term(factor, own, own_stat, packed_ref):
    rows = packed_ref.shape[0] - STAT_ROWS
    other = packed_ref[pl.ds(0, rows), :]
    pieces = packed_ref[pl.ds(rows, STAT_ROWS), :].astype(jnp.float32)
    other_stat = pieces[0:1, :] + (pieces[1:2, :] + pieces[2:3, :])
    scores = factor * lax.dot_general(
        own, other, (((1,), (1,)), ((), ())), preferred_element_type=jnp.float32
    )
    weights = (jnp.exp(scores - own_stat) + jnp.exp(scores - other_stat)).astype(jnp.bfloat16)
    return jnp.dot(weights, other, preferred_element_type=jnp.float32)


def first_kernel(factor_ref, own_ref, stat_ref, same_ref, pair_ref, out_ref):
    term = tile_term(factor_ref[0, 0], own_ref[...], stat_ref[...], same_ref)
    out_ref[...] = term - 2.0 * pair_ref[...].astype(jnp.float32)


def middle_kernel(factor_ref, own_ref, stat_ref, near_ref, far_ref, total_ref, out_ref):
    factor = factor_ref[0, 0]
    own, stat = own_ref[...], stat_ref[...]
    total = total_ref[...] + tile_term(factor, own, stat, near_ref)
    out_ref[...] = total + tile_term(factor, own, stat, far_ref)


def last_kernel(factor_ref, own_ref, stat_ref, both_ref, total_ref, out_ref):
    factor = factor_ref[0, 0]
    out_ref[...] = factor * (
        total_ref[...] + tile_term(factor, own_ref[...], stat_ref[...], both_ref)
    )


def call(kernel, flops, factor, own, stat, *arrays):
    rows, width = own.shape
    size = rows // BLOCKS
    blocked = pl.BlockSpec((size, width), lambda k: (k, 0))
    whole = pl.BlockSpec((rows + STAT_ROWS, width), lambda k: (0, 0))
    specs = [whole if a.shape[0] != rows else blocked for a in arrays]
    return pl.pallas_call(
        kernel,
        grid=(BLOCKS,),
        in_specs=[
            pl.BlockSpec(memory_space=pltpu.SMEM),
            blocked,
            pl.BlockSpec((size, 1), lambda k: (k, 0)),
            *specs,
        ],
        out_specs=blocked,
        out_shape=jax.ShapeDtypeStruct((rows, width), jnp.float32),
        compiler_params=pltpu.CompilerParams(vmem_limit_bytes=VMEM_BYTES),
        cost_estimate=pl.CostEstimate(
            flops=flops, bytes_accessed=flops // 1000, transcendentals=0
        ),
    )(factor, own, stat, *arrays)


def local(image_embeds, text_embeds, image_lse, text_lse, logit_scale):
    rows = image_embeds.shape[0]
    factor = logit_scale.reshape(1, 1)
    text, image = pack(text_embeds, text_lse, image_embeds, image_lse)
    far_text = shifted(text, "outer", 1)
    far_image = shifted(image, "outer", -1)
    near_text = shifted(text, "inner", 1)
    near_image = shifted(image, "inner", -1)

    on_images = (factor, image_embeds, image_lse.reshape(rows, 1))
    on_texts = (factor, text_embeds, text_lse.reshape(rows, 1))
    image_total = call(first_kernel, ON_IMAGES[0], *on_images, text, text_embeds)
    text_total = call(first_kernel, ON_TEXTS[0], *on_texts, image, image_embeds)
    far_text, image_total = lax.optimization_barrier((far_text, image_total))
    far_image, text_total = lax.optimization_barrier((far_image, text_total))
    both_text = shifted(far_text, "inner", 1)
    both_image = shifted(far_image, "inner", -1)
    image_total = call(middle_kernel, ON_IMAGES[1], *on_images, near_text, far_text, image_total)
    text_total = call(middle_kernel, ON_TEXTS[1], *on_texts, near_image, far_image, text_total)
    image_grad = call(last_kernel, ON_IMAGES[2], *on_images, both_text, image_total)
    both_image, image_grad = lax.optimization_barrier((both_image, image_grad))
    text_grad = call(last_kernel, ON_TEXTS[2], *on_texts, both_image, text_total)
    return (image_grad, text_grad)


def solution(mesh):
    return jax.shard_map(
        local,
        mesh=mesh,
        in_specs=(
            P(("outer", "inner"), None),
            P(("outer", "inner"), None),
            P(("outer", "inner")),
            P(("outer", "inner")),
            P(),
        ),
        out_specs=(P(("outer", "inner"), None), P(("outer", "inner"), None)),
        check_vma=False,
    )
```

```python
import jax
import jax.numpy as jnp
from jax import lax
from jax.experimental import pallas as pl
from jax.experimental.pallas import tpu as pltpu
from jax.sharding import PartitionSpec as P

STAT_ROWS = 16
BLOCKS = 4
VMEM_BYTES = 16 * 1024 * 1024
PACK_VMEM_BYTES = 8 * 1024 * 1024
COSTS = (2**29, 2**30, 2**29)


def shifted(value, axis, steps):
    count = lax.axis_size(axis)
    pairs = [(source, (source + steps) % count) for source in range(count)]
    return lax.ppermute(value, axis, pairs)


def pack_kernel(rows_ref, stat_ref, out, sem):
    rows = rows_ref.shape[0]
    copy = pltpu.make_async_copy(rows_ref, out.at[pl.ds(0, rows), :], sem)
    copy.start()
    stat = stat_ref[...]
    upper = stat.astype(jnp.bfloat16).astype(jnp.float32)
    rest = stat - upper
    middle = rest.astype(jnp.bfloat16).astype(jnp.float32)
    lower = rest - middle
    zeros = jnp.zeros((STAT_ROWS - 3, stat.shape[1]), jnp.float32)
    out[pl.ds(rows, STAT_ROWS), :] = jnp.concatenate(
        [upper, middle, lower, zeros], axis=0
    ).astype(jnp.bfloat16)
    copy.wait()


def pack(block, stat):
    rows, width = block.shape
    vmem = pl.BlockSpec(memory_space=pltpu.VMEM)
    return pl.pallas_call(
        pack_kernel,
        in_specs=[pl.BlockSpec(memory_space=pltpu.HBM), vmem],
        out_specs=vmem,
        out_shape=jax.ShapeDtypeStruct((rows + STAT_ROWS, width), jnp.bfloat16),
        scratch_shapes=[pltpu.SemaphoreType.DMA],
        compiler_params=pltpu.CompilerParams(vmem_limit_bytes=PACK_VMEM_BYTES),
    )(block, stat.reshape(1, rows))


def blocks(packed_ref):
    rows = packed_ref.shape[0] - STAT_ROWS
    size = rows // BLOCKS
    return [pl.ds(k * size, size) for k in range(BLOCKS)]


def tile_term(factor, own, own_stat, packed_ref):
    rows = packed_ref.shape[0] - STAT_ROWS
    other = packed_ref[pl.ds(0, rows), :]
    pieces = packed_ref[pl.ds(rows, STAT_ROWS), :].astype(jnp.float32)
    other_stat = pieces[0:1, :] + (pieces[1:2, :] + pieces[2:3, :])
    scores = factor * lax.dot_general(
        own, other, (((1,), (1,)), ((), ())), preferred_element_type=jnp.float32
    )
    weights = (jnp.exp(scores - own_stat) + jnp.exp(scores - other_stat)).astype(jnp.bfloat16)
    return jnp.dot(weights, other, preferred_element_type=jnp.float32)


def first_kernel(factor_ref, own_ref, stat_ref, pair_ref, out_ref):
    factor = factor_ref[0, 0]
    for cut in blocks(own_ref):
        term = tile_term(factor, own_ref[cut, :], stat_ref[cut, :], pair_ref)
        out_ref[cut, :] = term - 2.0 * pair_ref[cut, :].astype(jnp.float32)


def middle_kernel(factor_ref, own_ref, stat_ref, near_ref, far_ref, total_ref, out_ref):
    factor = factor_ref[0, 0]
    for cut in blocks(own_ref):
        own, stat = own_ref[cut, :], stat_ref[cut, :]
        total = total_ref[cut, :] + tile_term(factor, own, stat, near_ref)
        out_ref[cut, :] = total + tile_term(factor, own, stat, far_ref)


def last_kernel(factor_ref, own_ref, stat_ref, both_ref, total_ref, out_ref, done, sems):
    factor = factor_ref[0, 0]
    copies = []
    for k, cut in enumerate(blocks(own_ref)):
        term = tile_term(factor, own_ref[cut, :], stat_ref[cut, :], both_ref)
        done[cut, :] = factor * (total_ref[cut, :] + term)
        copies.append(pltpu.make_async_copy(done.at[cut, :], out_ref.at[cut, :], sems.at[k]))
        copies[k].start()
    for copy in copies:
        copy.wait()


def call(kernel, flops, factor, own, stat, *arrays):
    rows, width = stat.shape[0], own.shape[1]
    vmem = pl.BlockSpec(memory_space=pltpu.VMEM)
    last = kernel is last_kernel
    scratch = [pltpu.VMEM((rows, width), jnp.float32), pltpu.SemaphoreType.DMA((BLOCKS,))]
    return pl.pallas_call(
        kernel,
        in_specs=[pl.BlockSpec(memory_space=pltpu.SMEM)] + [vmem] * (2 + len(arrays)),
        out_specs=pl.BlockSpec(memory_space=pltpu.HBM) if last else vmem,
        out_shape=jax.ShapeDtypeStruct((rows, width), jnp.float32),
        scratch_shapes=scratch if last else [],
        compiler_params=pltpu.CompilerParams(vmem_limit_bytes=VMEM_BYTES),
        cost_estimate=pl.CostEstimate(
            flops=flops, bytes_accessed=flops // 1000, transcendentals=0
        ),
    )(factor, own, stat, *arrays)


def local(image_embeds, text_embeds, image_lse, text_lse, logit_scale):
    rows = image_embeds.shape[0]
    factor = logit_scale.reshape(1, 1)
    text = pack(text_embeds, text_lse)
    image = pack(image_embeds, image_lse)
    far_text = shifted(text, "outer", 1)
    far_image = shifted(image, "outer", -1)
    near_text = shifted(text, "inner", 1)
    near_image = shifted(image, "inner", -1)

    on_images = (factor, image, image_lse.reshape(rows, 1))
    on_texts = (factor, text, text_lse.reshape(rows, 1))
    image_total = call(first_kernel, COSTS[0], *on_images, text)
    text_total = call(first_kernel, COSTS[0], *on_texts, image)
    far_text, image_total = lax.optimization_barrier((far_text, image_total))
    far_image, text_total = lax.optimization_barrier((far_image, text_total))
    both_text = shifted(far_text, "inner", 1)
    both_image = shifted(far_image, "inner", -1)
    image_total = call(middle_kernel, COSTS[1], *on_images, near_text, far_text, image_total)
    text_total = call(middle_kernel, COSTS[1], *on_texts, near_image, far_image, text_total)
    image_grad = call(last_kernel, COSTS[2], *on_images, both_text, image_total)
    both_image, image_grad = lax.optimization_barrier((both_image, image_grad))
    text_grad = call(last_kernel, COSTS[2], *on_texts, both_image, text_total)
    return (image_grad, text_grad)


def solution(mesh):
    return jax.shard_map(
        local,
        mesh=mesh,
        in_specs=(
            P(("outer", "inner"), None),
            P(("outer", "inner"), None),
            P(("outer", "inner")),
            P(("outer", "inner")),
            P(),
        ),
        out_specs=(P(("outer", "inner"), None), P(("outer", "inner"), None)),
        check_vma=False,
    )
```

```python
import jax
import jax.numpy as jnp
from jax import lax
from jax.experimental import pallas as pl
from jax.experimental.pallas import tpu as pltpu
from jax.sharding import PartitionSpec as P

STAT_ROWS = 16
BLOCKS = 2
VMEM_BYTES = 16 * 1024 * 1024
PACK_VMEM_BYTES = 8 * 1024 * 1024
COSTS = (2**29, 2**29, 2**29, 2**29)


def shifted(value, axis, steps):
    count = lax.axis_size(axis)
    pairs = [(source, (source + steps) % count) for source in range(count)]
    return lax.ppermute(value, axis, pairs)


def pack_kernel(rows_ref, stat_ref, out, sem):
    rows = rows_ref.shape[0]
    copy = pltpu.make_async_copy(rows_ref, out.at[pl.ds(0, rows), :], sem)
    copy.start()
    stat = stat_ref[...]
    upper = stat.astype(jnp.bfloat16).astype(jnp.float32)
    rest = stat - upper
    middle = rest.astype(jnp.bfloat16).astype(jnp.float32)
    lower = rest - middle
    zeros = jnp.zeros((STAT_ROWS - 3, stat.shape[1]), jnp.float32)
    out[pl.ds(rows, STAT_ROWS), :] = jnp.concatenate(
        [upper, middle, lower, zeros], axis=0
    ).astype(jnp.bfloat16)
    copy.wait()


def pack(block, stat):
    rows, width = block.shape
    vmem = pl.BlockSpec(memory_space=pltpu.VMEM)
    return pl.pallas_call(
        pack_kernel,
        in_specs=[pl.BlockSpec(memory_space=pltpu.HBM), vmem],
        out_specs=vmem,
        out_shape=jax.ShapeDtypeStruct((rows + STAT_ROWS, width), jnp.bfloat16),
        scratch_shapes=[pltpu.SemaphoreType.DMA],
        compiler_params=pltpu.CompilerParams(vmem_limit_bytes=PACK_VMEM_BYTES),
    )(block, stat.reshape(1, rows))


def blocks(packed_ref):
    rows = packed_ref.shape[0] - STAT_ROWS
    size = rows // BLOCKS
    return [pl.ds(k * size, size) for k in range(BLOCKS)]


def tile_weights(factor, own, own_stat, packed_ref):
    rows = packed_ref.shape[0] - STAT_ROWS
    pieces = packed_ref[pl.ds(rows, STAT_ROWS), :].astype(jnp.float32)
    other_stat = pieces[0:1, :] + (pieces[1:2, :] + pieces[2:3, :])
    scores = factor * lax.dot_general(
        own,
        packed_ref[pl.ds(0, rows), :],
        (((1,), (1,)), ((), ())),
        preferred_element_type=jnp.float32,
    )
    return (jnp.exp(scores - own_stat) + jnp.exp(scores - other_stat)).astype(jnp.bfloat16)


def tile_term(factor, own, own_stat, packed_ref):
    rows = packed_ref.shape[0] - STAT_ROWS
    weights = tile_weights(factor, own, own_stat, packed_ref)
    return jnp.dot(weights, packed_ref[pl.ds(0, rows), :], preferred_element_type=jnp.float32)


def first_kernel(factor_ref, own_ref, stat_ref, pair_ref, out_ref):
    factor = factor_ref[0, 0]
    for cut in blocks(own_ref):
        term = tile_term(factor, own_ref[cut, :], stat_ref[cut, :], pair_ref)
        out_ref[cut, :] = term - 2.0 * pair_ref[cut, :].astype(jnp.float32)


def middle_kernel(factor_ref, own_ref, stat_ref, other_ref, total_ref, out_ref):
    factor = factor_ref[0, 0]
    for cut in blocks(own_ref):
        term = tile_term(factor, own_ref[cut, :], stat_ref[cut, :], other_ref)
        out_ref[cut, :] = total_ref[cut, :] + term


def last_kernel(factor_ref, own_ref, stat_ref, both_ref, total_ref, out_ref, done, sems):
    factor = factor_ref[0, 0]
    rows, width = done.shape
    copies = []
    for k, cut in enumerate(blocks(own_ref)):
        weights = tile_weights(factor, own_ref[cut, :], stat_ref[cut, :], both_ref)
        for half in range(2):
            part = pl.ds(half * (width // 2), width // 2)
            term = jnp.dot(
                weights, both_ref[pl.ds(0, rows), part], preferred_element_type=jnp.float32
            )
            done[cut, part] = factor * (total_ref[cut, part] + term)
            copy = pltpu.make_async_copy(
                done.at[cut, part], out_ref.at[cut, part], sems.at[2 * k + half]
            )
            copy.start()
            copies.append(copy)
    for copy in copies:
        copy.wait()


def call(kernel, flops, factor, own, stat, *arrays):
    rows, width = stat.shape[0], own.shape[1]
    vmem = pl.BlockSpec(memory_space=pltpu.VMEM)
    last = kernel is last_kernel
    scratch = [pltpu.VMEM((rows, width), jnp.float32), pltpu.SemaphoreType.DMA((2 * BLOCKS,))]
    return pl.pallas_call(
        kernel,
        in_specs=[pl.BlockSpec(memory_space=pltpu.SMEM)] + [vmem] * (2 + len(arrays)),
        out_specs=pl.BlockSpec(memory_space=pltpu.HBM) if last else vmem,
        out_shape=jax.ShapeDtypeStruct((rows, width), jnp.float32),
        scratch_shapes=scratch if last else [],
        compiler_params=pltpu.CompilerParams(vmem_limit_bytes=VMEM_BYTES),
        cost_estimate=pl.CostEstimate(
            flops=flops, bytes_accessed=flops // 1000, transcendentals=0
        ),
    )(factor, own, stat, *arrays)


def local(image_embeds, text_embeds, image_lse, text_lse, logit_scale):
    rows = image_embeds.shape[0]
    factor = logit_scale.reshape(1, 1)
    text = pack(text_embeds, text_lse)
    image = pack(image_embeds, image_lse)
    far_text = shifted(text, "outer", 1)
    far_image = shifted(image, "outer", -1)
    near_text = shifted(text, "inner", 1)
    near_image = shifted(image, "inner", -1)

    on_images = (factor, image, image_lse.reshape(rows, 1))
    on_texts = (factor, text, text_lse.reshape(rows, 1))
    image_total = call(first_kernel, COSTS[0], *on_images, text)
    text_total = call(first_kernel, COSTS[0], *on_texts, image)
    far_text, image_total = lax.optimization_barrier((far_text, image_total))
    both_text = shifted(far_text, "inner", 1)
    image_total = call(middle_kernel, COSTS[1], *on_images, far_text, image_total)
    far_image, image_total, text_total = lax.optimization_barrier(
        (far_image, image_total, text_total)
    )
    both_image = shifted(far_image, "inner", -1)
    image_total = call(middle_kernel, COSTS[1], *on_images, near_text, image_total)
    text_total = call(middle_kernel, COSTS[1], *on_texts, near_image, text_total)
    text_total = call(middle_kernel, COSTS[2], *on_texts, far_image, text_total)
    image_grad = call(last_kernel, COSTS[3], *on_images, both_text, image_total)
    both_image, image_grad = lax.optimization_barrier((both_image, image_grad))
    text_grad = call(last_kernel, COSTS[3], *on_texts, both_image, text_total)
    return (image_grad, text_grad)


def solution(mesh):
    return jax.shard_map(
        local,
        mesh=mesh,
        in_specs=(
            P(("outer", "inner"), None),
            P(("outer", "inner"), None),
            P(("outer", "inner")),
            P(("outer", "inner")),
            P(),
        ),
        out_specs=(P(("outer", "inner"), None), P(("outer", "inner"), None)),
        check_vma=False,
    )
```

```python
import jax
import jax.numpy as jnp
from jax import lax
from jax.experimental import pallas as pl
from jax.experimental.pallas import tpu as pltpu
from jax.sharding import PartitionSpec as P

STAT_ROWS = 16
BLOCKS = 2
VMEM_BYTES = 16 * 1024 * 1024
PACK_VMEM_BYTES = 8 * 1024 * 1024
COSTS = (2**29, 2**29, 2**29, 2**29)


def shifted(value, axis, steps):
    count = lax.axis_size(axis)
    pairs = [(source, (source + steps) % count) for source in range(count)]
    return lax.ppermute(value, axis, pairs)


def pack_kernel(rows_ref, stat_ref, out, sem):
    rows = rows_ref.shape[0]
    copy = pltpu.make_async_copy(rows_ref, out.at[pl.ds(0, rows), :], sem)
    copy.start()
    stat = stat_ref[...]
    upper = stat.astype(jnp.bfloat16).astype(jnp.float32)
    rest = stat - upper
    middle = rest.astype(jnp.bfloat16).astype(jnp.float32)
    lower = rest - middle
    zeros = jnp.zeros((STAT_ROWS - 3, stat.shape[1]), jnp.float32)
    out[pl.ds(rows, STAT_ROWS), :] = jnp.concatenate(
        [upper, middle, lower, zeros], axis=0
    ).astype(jnp.bfloat16)
    copy.wait()


def pack(block, stat):
    rows, width = block.shape
    vmem = pl.BlockSpec(memory_space=pltpu.VMEM)
    return pl.pallas_call(
        pack_kernel,
        in_specs=[pl.BlockSpec(memory_space=pltpu.HBM), vmem],
        out_specs=vmem,
        out_shape=jax.ShapeDtypeStruct((rows + STAT_ROWS, width), jnp.bfloat16),
        scratch_shapes=[pltpu.SemaphoreType.DMA],
        compiler_params=pltpu.CompilerParams(vmem_limit_bytes=PACK_VMEM_BYTES),
    )(block, stat.reshape(1, rows))


def blocks(packed_ref):
    rows = packed_ref.shape[0] - STAT_ROWS
    size = rows // BLOCKS
    return [pl.ds(k * size, size) for k in range(BLOCKS)]


def tile_weights(factor, own, own_stat, packed_ref):
    rows = packed_ref.shape[0] - STAT_ROWS
    pieces = packed_ref[pl.ds(rows, STAT_ROWS), :].astype(jnp.float32)
    other_stat = pieces[0:1, :] + (pieces[1:2, :] + pieces[2:3, :])
    scores = factor * lax.dot_general(
        own,
        packed_ref[pl.ds(0, rows), :],
        (((1,), (1,)), ((), ())),
        preferred_element_type=jnp.float32,
    )
    return (jnp.exp(scores - own_stat) + jnp.exp(scores - other_stat)).astype(jnp.bfloat16)


def tile_term(factor, own, own_stat, packed_ref):
    rows = packed_ref.shape[0] - STAT_ROWS
    weights = tile_weights(factor, own, own_stat, packed_ref)
    return jnp.dot(weights, packed_ref[pl.ds(0, rows), :], preferred_element_type=jnp.float32)


def first_kernel(factor_ref, own_ref, stat_ref, pair_ref, out_ref):
    factor = factor_ref[0, 0]
    for cut in blocks(own_ref):
        term = tile_term(factor, own_ref[cut, :], stat_ref[cut, :], pair_ref)
        out_ref[cut, :] = term - 2.0 * pair_ref[cut, :].astype(jnp.float32)


def middle_kernel(factor_ref, own_ref, stat_ref, other_ref, total_ref, out_ref):
    factor = factor_ref[0, 0]
    for cut in blocks(own_ref):
        term = tile_term(factor, own_ref[cut, :], stat_ref[cut, :], other_ref)
        out_ref[cut, :] = total_ref[cut, :] + term


def last_kernel(factor_ref, own_ref, stat_ref, both_ref, total_ref, out_ref, done, sems):
    factor = factor_ref[0, 0]
    rows, width = done.shape
    copies = []
    for k, cut in enumerate(blocks(own_ref)):
        weights = tile_weights(factor, own_ref[cut, :], stat_ref[cut, :], both_ref)
        for half in range(2):
            part = pl.ds(half * (width // 2), width // 2)
            term = jnp.dot(
                weights, both_ref[pl.ds(0, rows), part], preferred_element_type=jnp.float32
            )
            done[cut, part] = factor * (total_ref[cut, part] + term)
            copy = pltpu.make_async_copy(
                done.at[cut, part], out_ref.at[cut, part], sems.at[2 * k + half]
            )
            copy.start()
            copies.append(copy)
    for copy in copies:
        copy.wait()


def call(kernel, flops, factor, own, stat, *arrays):
    rows, width = stat.shape[0], own.shape[1]
    vmem = pl.BlockSpec(memory_space=pltpu.VMEM)
    last = kernel is last_kernel
    scratch = [pltpu.VMEM((rows, width), jnp.float32), pltpu.SemaphoreType.DMA((2 * BLOCKS,))]
    return pl.pallas_call(
        kernel,
        in_specs=[pl.BlockSpec(memory_space=pltpu.SMEM)] + [vmem] * (2 + len(arrays)),
        out_specs=pl.BlockSpec(memory_space=pltpu.HBM) if last else vmem,
        out_shape=jax.ShapeDtypeStruct((rows, width), jnp.float32),
        scratch_shapes=scratch if last else [],
        compiler_params=pltpu.CompilerParams(vmem_limit_bytes=VMEM_BYTES),
        cost_estimate=pl.CostEstimate(
            flops=flops, bytes_accessed=flops // 1000, transcendentals=0
        ),
    )(factor, own, stat, *arrays)


def local(image_embeds, text_embeds, image_lse, text_lse, logit_scale):
    rows = image_embeds.shape[0]
    factor = logit_scale.reshape(1, 1)
    text = pack(text_embeds, text_lse)
    image = pack(image_embeds, image_lse)
    far_text = shifted(text, "outer", 1)
    far_image = shifted(image, "outer", -1)
    near_text = shifted(text, "inner", 1)
    near_image = shifted(image, "inner", -1)

    on_images = (factor, image, image_lse.reshape(rows, 1))
    on_texts = (factor, text, text_lse.reshape(rows, 1))
    image_total = call(first_kernel, COSTS[0], *on_images, text)
    text_total = call(first_kernel, COSTS[0], *on_texts, image)
    far_text, image_total, text_total = lax.optimization_barrier(
        (far_text, image_total, text_total)
    )
    both_text = shifted(far_text, "inner", 1)
    both_image = shifted(far_image, "inner", -1)
    image_total = call(middle_kernel, COSTS[1], *on_images, near_text, image_total)
    text_total = call(middle_kernel, COSTS[1], *on_texts, near_image, text_total)
    image_total = call(middle_kernel, COSTS[1], *on_images, far_text, image_total)
    text_total = call(middle_kernel, COSTS[1], *on_texts, far_image, text_total)
    image_grad = call(last_kernel, COSTS[3], *on_images, both_text, image_total)
    both_image, image_grad = lax.optimization_barrier((both_image, image_grad))
    text_grad = call(last_kernel, COSTS[3], *on_texts, both_image, text_total)
    return (image_grad, text_grad)


def solution(mesh):
    return jax.shard_map(
        local,
        mesh=mesh,
        in_specs=(
            P(("outer", "inner"), None),
            P(("outer", "inner"), None),
            P(("outer", "inner")),
            P(("outer", "inner")),
            P(),
        ),
        out_specs=(P(("outer", "inner"), None), P(("outer", "inner"), None)),
        check_vma=False,
    )
```

```python
import jax
import jax.numpy as jnp
from jax import lax
from jax.experimental import pallas as pl
from jax.experimental.pallas import tpu as pltpu
from jax.sharding import PartitionSpec as P

STAT_ROWS = 16
BLOCKS = 2
VMEM_BYTES = 16 * 1024 * 1024
PIECES = 4
PACK_VMEM_BYTES = 60 * 1024 * 1024
COSTS = (2**29, 2**29, 2**29, 2**29)


def shifted(value, axis, steps):
    count = lax.axis_size(axis)
    pairs = [(source, (source + steps) % count) for source in range(count)]
    return lax.ppermute(value, axis, pairs)


def pack_kernel(rows_ref, stat_ref, out, held, sems):
    rows = rows_ref.shape[0]
    size = rows // PIECES
    cuts = [pl.ds(k * size, size) for k in range(PIECES)]
    loads = [
        pltpu.make_async_copy(rows_ref.at[cut, :], held.at[cut, :], sems.at[0, k])
        for k, cut in enumerate(cuts)
    ]
    cuts.append(pl.ds(rows, STAT_ROWS))
    stores = [
        pltpu.make_async_copy(held.at[cut, :], out.at[cut, :], sems.at[1, k])
        for k, cut in enumerate(cuts)
    ]
    for load in loads:
        load.start()
    stat = stat_ref[...]
    upper = stat.astype(jnp.bfloat16).astype(jnp.float32)
    rest = stat - upper
    middle = rest.astype(jnp.bfloat16).astype(jnp.float32)
    lower = rest - middle
    zeros = jnp.zeros((STAT_ROWS - 3, stat.shape[1]), jnp.float32)
    held[pl.ds(rows, STAT_ROWS), :] = jnp.concatenate(
        [upper, middle, lower, zeros], axis=0
    ).astype(jnp.bfloat16)
    stores[PIECES].start()
    for k in range(PIECES):
        loads[k].wait()
        stores[k].start()
    for store in stores:
        store.wait()


def pack(block, stat):
    rows, width = block.shape
    hbm = pl.BlockSpec(memory_space=pltpu.HBM)
    return pl.pallas_call(
        pack_kernel,
        in_specs=[hbm, pl.BlockSpec(memory_space=pltpu.VMEM)],
        out_specs=hbm,
        out_shape=jax.ShapeDtypeStruct((rows + STAT_ROWS, width), jnp.bfloat16),
        scratch_shapes=[
            pltpu.VMEM((rows + STAT_ROWS, width), jnp.bfloat16),
            pltpu.SemaphoreType.DMA((2, PIECES + 1)),
        ],
        compiler_params=pltpu.CompilerParams(vmem_limit_bytes=PACK_VMEM_BYTES),
    )(block, stat.reshape(1, rows))


def blocks(packed_ref):
    rows = packed_ref.shape[0] - STAT_ROWS
    size = rows // BLOCKS
    return [pl.ds(k * size, size) for k in range(BLOCKS)]


def tile_weights(factor, own, own_stat, packed_ref):
    rows = packed_ref.shape[0] - STAT_ROWS
    pieces = packed_ref[pl.ds(rows, STAT_ROWS), :].astype(jnp.float32)
    other_stat = pieces[0:1, :] + (pieces[1:2, :] + pieces[2:3, :])
    scores = factor * lax.dot_general(
        own,
        packed_ref[pl.ds(0, rows), :],
        (((1,), (1,)), ((), ())),
        preferred_element_type=jnp.float32,
    )
    return (jnp.exp(scores - own_stat) + jnp.exp(scores - other_stat)).astype(jnp.bfloat16)


def tile_term(factor, own, own_stat, packed_ref):
    rows = packed_ref.shape[0] - STAT_ROWS
    weights = tile_weights(factor, own, own_stat, packed_ref)
    return jnp.dot(weights, packed_ref[pl.ds(0, rows), :], preferred_element_type=jnp.float32)


def first_kernel(factor_ref, own_ref, stat_ref, pair_ref, out_ref):
    factor = factor_ref[0, 0]
    for cut in blocks(own_ref):
        term = tile_term(factor, own_ref[cut, :], stat_ref[cut, :], pair_ref)
        out_ref[cut, :] = term - 2.0 * pair_ref[cut, :].astype(jnp.float32)


def middle_kernel(factor_ref, own_ref, stat_ref, other_ref, total_ref, out_ref):
    factor = factor_ref[0, 0]
    for cut in blocks(own_ref):
        term = tile_term(factor, own_ref[cut, :], stat_ref[cut, :], other_ref)
        out_ref[cut, :] = total_ref[cut, :] + term


def last_kernel(factor_ref, own_ref, stat_ref, both_ref, total_ref, out_ref, done, sems):
    factor = factor_ref[0, 0]
    rows, width = done.shape
    copies = []
    for k, cut in enumerate(blocks(own_ref)):
        weights = tile_weights(factor, own_ref[cut, :], stat_ref[cut, :], both_ref)
        for half in range(2):
            part = pl.ds(half * (width // 2), width // 2)
            term = jnp.dot(
                weights, both_ref[pl.ds(0, rows), part], preferred_element_type=jnp.float32
            )
            done[cut, part] = factor * (total_ref[cut, part] + term)
            copy = pltpu.make_async_copy(
                done.at[cut, part], out_ref.at[cut, part], sems.at[2 * k + half]
            )
            copy.start()
            copies.append(copy)
    for copy in copies:
        copy.wait()


def call(kernel, flops, factor, own, stat, *arrays):
    rows, width = stat.shape[0], own.shape[1]
    vmem = pl.BlockSpec(memory_space=pltpu.VMEM)
    last = kernel is last_kernel
    scratch = [pltpu.VMEM((rows, width), jnp.float32), pltpu.SemaphoreType.DMA((2 * BLOCKS,))]
    return pl.pallas_call(
        kernel,
        in_specs=[pl.BlockSpec(memory_space=pltpu.SMEM)] + [vmem] * (2 + len(arrays)),
        out_specs=pl.BlockSpec(memory_space=pltpu.HBM) if last else vmem,
        out_shape=jax.ShapeDtypeStruct((rows, width), jnp.float32),
        scratch_shapes=scratch if last else [],
        compiler_params=pltpu.CompilerParams(vmem_limit_bytes=VMEM_BYTES),
        cost_estimate=pl.CostEstimate(
            flops=flops, bytes_accessed=flops // 1000, transcendentals=0
        ),
    )(factor, own, stat, *arrays)


def local(image_embeds, text_embeds, image_lse, text_lse, logit_scale):
    rows = image_embeds.shape[0]
    factor = logit_scale.reshape(1, 1)
    text = pack(text_embeds, text_lse)
    image = pack(image_embeds, image_lse)
    far_text = shifted(text, "outer", 1)
    far_image = shifted(image, "outer", -1)
    near_text = shifted(text, "inner", 1)
    near_image = shifted(image, "inner", -1)

    on_images = (factor, image, image_lse.reshape(rows, 1))
    on_texts = (factor, text, text_lse.reshape(rows, 1))
    image_total = call(first_kernel, COSTS[0], *on_images, text)
    text_total = call(first_kernel, COSTS[0], *on_texts, image)
    far_text, image_total = lax.optimization_barrier((far_text, image_total))
    both_text = shifted(far_text, "inner", 1)
    image_total = call(middle_kernel, COSTS[1], *on_images, far_text, image_total)
    far_image, image_total, text_total = lax.optimization_barrier(
        (far_image, image_total, text_total)
    )
    both_image = shifted(far_image, "inner", -1)
    image_total = call(middle_kernel, COSTS[1], *on_images, near_text, image_total)
    text_total = call(middle_kernel, COSTS[1], *on_texts, near_image, text_total)
    text_total = call(middle_kernel, COSTS[2], *on_texts, far_image, text_total)
    image_grad = call(last_kernel, COSTS[3], *on_images, both_text, image_total)
    both_image, image_grad = lax.optimization_barrier((both_image, image_grad))
    text_grad = call(last_kernel, COSTS[3], *on_texts, both_image, text_total)
    return (image_grad, text_grad)


def solution(mesh):
    return jax.shard_map(
        local,
        mesh=mesh,
        in_specs=(
            P(("outer", "inner"), None),
            P(("outer", "inner"), None),
            P(("outer", "inner")),
            P(("outer", "inner")),
            P(),
        ),
        out_specs=(P(("outer", "inner"), None), P(("outer", "inner"), None)),
        check_vma=False,
    )
```
